32 devices in a mesh: grp: 4 (over y, x), seq: 8 (over z, core).
Axes of the slice: x: 2, y: 2, z: 4, core: 2. Of those that a mesh axis runs over, the one named last changes fastest.
Arguments:
- queries: bfloat16 [4, 1024, 2048], P('grp', 'seq'), may hold values from -6 to 6
- keys: bfloat16 [4, 1024, 512], P('grp', 'seq'), may hold values from -6 to 6
- values: bfloat16 [4, 1024, 512], P('grp', 'seq'), may hold values from -6 to 6
- route_ids: int32 [4, 1024, 8], P('grp', 'seq'), may hold values from 0 to 31, all different within a row; in each aligned block of 128 rows (0 to 127, 128 to 255, ..., all dimensions but the last counted through in order) at most 36 rows name the same one
- route_weights: float32 [4, 1024, 8], P('grp', 'seq'), may hold values from 0.05 to 0.3
- out_weight: bfloat16 [2048, 2048], replicated, may hold values from -1.5909903 to 1.5909903
- norm_gain: float32 [2048], replicated, may hold values from 0.5 to 1.5
- gate_up: bfloat16 [32, 2048, 1536], P(('grp', 'seq')), may hold values from -0.125 to 0.125
- down_weight: bfloat16 [32, 768, 2048], P(('grp', 'seq')), may hold values from -0.21875 to 0.21875
Outputs:
- mixed: bfloat16 [4, 1024, 2048], P('grp', 'seq')
The draws below stay inside these ranges and needn't reach their ends.
Inputs may be any that keep to these rules, and one draw needn't show every extreme that they name: `route_ids`: each row names 8 different experts; the rows of one device name no expert more than 36 times, and in some devices' rows some expert exactly 36 times.
All inputs are finite; a program needn't handle non-finite values.
Results may differ from the reference program's by a relative error of at most 0.008.
Values may be sent and summed in bfloat16 or wider, within the bound.
A program may use at most 128 MiB of HBM per device.

```python
import math
import jax
import jax.numpy as jnp
import numpy as np
from jax import lax

D = 2048
QUERY_HEADS = 16
KEY_VALUE_HEADS = 4
HEAD_WIDTH = 128
FF = 768
TOP = 8
TOK_DEV = 128
EXPERTS = 32
CAP = 36
SEQUENCE_COUNT = 4
TOKEN_LENGTH = 1024
N_GRP = 4
N_SEQ = 8


def draw_queries(key, part):
    input_source = jax.random.fold_in(key, 3)
    start_offset = jnp.clip(jax.random.normal(input_source, (SEQUENCE_COUNT, TOKEN_LENGTH, QUERY_HEADS, HEAD_WIDTH)), -6.0, 6.0)
    return start_offset.reshape(SEQUENCE_COUNT, TOKEN_LENGTH, QUERY_HEADS * HEAD_WIDTH).astype(jnp.bfloat16)


def draw_keys(key, part):
    input_source = jax.random.fold_in(key, 5)
    start_offset = jnp.clip(jax.random.normal(input_source, (SEQUENCE_COUNT, TOKEN_LENGTH, KEY_VALUE_HEADS, HEAD_WIDTH)), -6.0, 6.0)
    return start_offset.reshape(SEQUENCE_COUNT, TOKEN_LENGTH, KEY_VALUE_HEADS * HEAD_WIDTH).astype(jnp.bfloat16)


def draw_out_weight(key, part):
    first_operand, second_operand, third = jax.random.split(jax.random.fold_in(key, 9), 3)
    lower, upper = (0.5, 2.0)
    row_scale = jnp.exp(jax.random.uniform(second_operand, (QUERY_HEADS * HEAD_WIDTH, 1), minval=math.log(lower), maxval=math.log(upper)))
    col_scale = jnp.exp(jax.random.uniform(third, (1, D), minval=math.log(lower), maxval=math.log(upper)))
    start_offset = jnp.clip(jax.random.normal(first_operand, (QUERY_HEADS * HEAD_WIDTH, D)), -4.0, 4.0) * 2.0 / math.sqrt(QUERY_HEADS * HEAD_WIDTH)
    return (start_offset * row_scale * col_scale).astype(jnp.bfloat16)


def levels(key, extent, cuts, least, high):
    level = 1.0
    for dim, shards_of in cuts:
        draws = jax.random.uniform(jax.random.fold_in(jax.random.fold_in(key, 6), dim), (shards_of,), jnp.float32, least / len(cuts), high / len(cuts))
        level = level * jnp.repeat(jnp.exp(draws), extent[dim] // shards_of).reshape((-1,) + (1,) * (len(extent) - 1 - dim))
    return level


def shared_out(rng, own, number, rows, amount, top, limit, skew):
    order = jax.random.permutation(rng, amount)
    crowded, ordinary = load_shares(amount, rows * top, limit, skew, True), load_shares(amount, rows * top, limit, skew, False)
    places = jnp.arange(amount)

    def named(sizes, rotation):
        used = int((sizes > 0).sum())
        fixed = max(1, used // 4)
        shifted = fixed + (places - fixed + rotation * (used - fixed)) % max(1, amount - fixed)
        return jnp.zeros((amount,), jnp.int32).at[order[jnp.where(places < fixed, places, shifted)]].set(jnp.asarray(sizes, jnp.int32))

    sizes = jnp.where(number % 4 == 0, named(crowded, number // 4), named(ordinary, number - number // 4 - 1))
    mixed = jax.random.permutation(jax.random.fold_in(own, 3), amount)
    donor, sink = mixed[0:amount // 2 * 2:2], mixed[1:amount // 2 * 2:2]
    slack = jnp.minimum(sizes[donor] - 1, limit - sizes[sink]) // 2
    slack = jnp.where((donor == order[0]) | (sink == order[0]) | (sizes[sink] == 0), 0, jnp.maximum(slack, 0))
    shifted = jax.random.randint(jax.random.fold_in(own, 4), (amount // 2,), 0, 1 << 20) % (slack + 1)
    sizes = sizes.at[donor].add(-shifted).at[sink].add(shifted)
    items = jnp.searchsorted(jnp.cumsum(sizes), jnp.arange(rows * top), side="right").astype(jnp.int32)
    grid = items.reshape(top, rows).T
    grid = grid[jax.random.permutation(jax.random.fold_in(own, 1), rows)]
    rotation = jax.random.randint(jax.random.fold_in(own, 2), (rows, 1), 0, top)
    return jnp.take_along_axis(grid, (jnp.arange(top)[None, :] + rotation) % top, axis=1)


def load_shares(count, total, limit, lean, full):
    weights = [(1 << 20) // math.isqrt(rank ** lean) + 1 for rank in range(1, count + 1)]
    largest = limit if full else min(limit, max(-(-total // count), total * weights[0] // sum(weights)))
    least = 1 if total - largest >= count - 1 else 0
    given, rest = [largest] + [least] * (count - 1), total - largest - least * (count - 1)
    while rest > 0:
        free = [i for i in range(1, count) if given[i] < largest] or [i for i in range(1, count) if given[i] < limit]
        whole, remaining = sum([weights[i] for i in free]), rest
        for i in free:
            addition = min(limit - given[i], max(1, remaining * weights[i] // whole), rest)
            given[i] = given[i] + addition
            rest = rest - addition
    return np.array(given)


def bell_draw(stream_key, shape, scale, bound, cuts=(), held_as=jnp.bfloat16):
    loudness = levels(stream_key, shape, cuts, -0.22, 0.18) if cuts else 1.0
    drawn = jax.random.normal(stream_key, shape, jnp.float32) * scale * loudness
    return jnp.minimum(jnp.maximum(drawn, -bound), bound).astype(held_as)


def setup_inputs(seed: int = 0) -> dict:
    arg_keys = jax.random.split(jax.random.key(seed), 10)
    queries = draw_queries(jax.random.fold_in(arg_keys[9], 71), 0)
    keys = draw_keys(jax.random.fold_in(arg_keys[9], 71), 0)
    values = bell_draw(arg_keys[2], (SEQUENCE_COUNT, TOKEN_LENGTH, KEY_VALUE_HEADS * HEAD_WIDTH), 1.0, 6.0, ((0, 4), (1, 8)))
    route_ids_keys = jax.random.split(jax.random.fold_in(arg_keys[3], 1), SEQUENCE_COUNT * TOKEN_LENGTH // TOK_DEV)
    route_ids_turns = jax.random.permutation(jax.random.fold_in(arg_keys[3], 3), SEQUENCE_COUNT * TOKEN_LENGTH // TOK_DEV)
    route_ids = jax.vmap(lambda own, number: shared_out(jax.random.fold_in(arg_keys[3], 2), own, number, TOK_DEV, EXPERTS, TOP, CAP, 1))(route_ids_keys, route_ids_turns).reshape((SEQUENCE_COUNT, TOKEN_LENGTH, TOP))
    route_weights = jnp.clip(0.05 + 0.25 * jax.random.uniform(arg_keys[4], (SEQUENCE_COUNT, TOKEN_LENGTH, TOP), jnp.float32) ** levels(arg_keys[4], (SEQUENCE_COUNT, TOKEN_LENGTH, TOP), ((0, 4), (1, 8)), -0.2, 0.2), 0.05, 0.3)
    out_weight = draw_out_weight(jax.random.fold_in(arg_keys[9], 71), 0)
    norm_gain = jnp.clip(1.0 + 0.1 * jax.random.normal(arg_keys[6], (D,), jnp.float32), 0.5, 1.5)
    gate_up = bell_draw(arg_keys[7], (EXPERTS, D, 2 * FF), D ** -0.5, 0.125, ((0, 32),))
    down_weight = bell_draw(arg_keys[8], (EXPERTS, FF, D), FF ** -0.5, 0.21875, ((0, 32),))
    return {"queries": queries, "keys": keys, "values": values, "route_ids": route_ids, "route_weights": route_weights, "out_weight": out_weight, "norm_gain": norm_gain, "gate_up": gate_up, "down_weight": down_weight}


def normalize_rows(scores):
    highest = lax.optimization_barrier(jnp.max(scores, axis=-1, keepdims=True))
    raised = jnp.exp(scores - highest)
    return (raised / lax.optimization_barrier(jnp.sum(raised, axis=-1, keepdims=True))).astype(jnp.bfloat16)

def head_attention(packed):
    query, key_rows, value_rows = packed
    token_length = query.shape[0]
    scores = jnp.dot(query, key_rows.T, preferred_element_type=jnp.float32) * HEAD_WIDTH ** (-0.5)
    row_index = jnp.arange(token_length, dtype=jnp.int32)[:, None]
    col_index = jnp.arange(token_length, dtype=jnp.int32)[None, :]
    scores = jnp.where(col_index <= row_index, scores, -jnp.inf)
    return jnp.dot(normalize_rows(scores), value_rows, preferred_element_type=jnp.float32).astype(jnp.bfloat16)

def slot_numbers(block):
    onehot = (block[:, None] == jnp.arange(EXPERTS, dtype=jnp.int32)[None, :]).astype(jnp.int32)
    before = jnp.cumsum(onehot, axis=0) - onehot
    return lax.optimization_barrier(jnp.sum(before * onehot, axis=1)).astype(jnp.int32)

def reference(queries, keys, values, route_ids, route_weights, out_weight, norm_gain, gate_up, down_weight):
    sequence_total, token_length = (queries.shape[0], queries.shape[1])
    heads_per_group = QUERY_HEADS // KEY_VALUE_HEADS
    q_heads = queries.reshape(sequence_total, token_length, QUERY_HEADS, HEAD_WIDTH).transpose(0, 2, 1, 3).reshape(sequence_total * QUERY_HEADS, token_length, HEAD_WIDTH)
    key_heads = jnp.repeat(keys.reshape(sequence_total, token_length, KEY_VALUE_HEADS, HEAD_WIDTH).transpose(0, 2, 1, 3), heads_per_group, axis=1)
    key_heads = key_heads.reshape(sequence_total * QUERY_HEADS, token_length, HEAD_WIDTH)
    value_heads = jnp.repeat(values.reshape(sequence_total, token_length, KEY_VALUE_HEADS, HEAD_WIDTH).transpose(0, 2, 1, 3), heads_per_group, axis=1)
    value_heads = value_heads.reshape(sequence_total * QUERY_HEADS, token_length, HEAD_WIDTH)
    attended = lax.map(head_attention, (q_heads, key_heads, value_heads))
    attended = attended.reshape(sequence_total, QUERY_HEADS, token_length, HEAD_WIDTH).transpose(0, 2, 1, 3).reshape(sequence_total * token_length, QUERY_HEADS * HEAD_WIDTH)
    hidden_state = jnp.dot(attended, out_weight, preferred_element_type=jnp.float32)
    power = lax.optimization_barrier(jnp.mean(hidden_state * hidden_state, axis=-1, keepdims=True))
    normed = (hidden_state * lax.rsqrt(power + 1e-06) * norm_gain).astype(jnp.bfloat16)
    total = sequence_total * token_length
    devices = N_GRP * N_SEQ
    routes = TOK_DEV * TOP
    flat_ids = route_ids.reshape(devices, routes).astype(jnp.int32)
    slots = jax.vmap(slot_numbers)(flat_ids)
    target = flat_ids * CAP + slots
    owners = jnp.arange(devices, dtype=jnp.int32)[:, None] * TOK_DEV + jnp.arange(routes, dtype=jnp.int32)[None, :] // TOP
    row_select = jnp.broadcast_to(jnp.arange(devices, dtype=jnp.int32)[:, None], target.shape)
    table = jnp.full((devices, EXPERTS * CAP), total, jnp.int32).at[row_select, target].set(owners)
    shares = jnp.zeros((devices, EXPERTS * CAP), jnp.float32).at[row_select, target].set(route_weights.reshape(devices, routes).astype(jnp.float32))
    table = table.reshape(devices, EXPERTS, CAP).transpose(1, 0, 2).reshape(EXPERTS, devices * CAP)
    shares = shares.reshape(devices, EXPERTS, CAP).transpose(1, 0, 2).reshape(EXPERTS, devices * CAP)
    padded = jnp.concatenate([normed, jnp.zeros((1, D), jnp.bfloat16)], axis=0)

    def expert_step(summed, packed):
        table_row, share_row, gate_part, down_part = packed
        picked = padded[table_row]
        both = jnp.dot(picked, gate_part, preferred_element_type=jnp.float32)
        inner = (jax.nn.silu(both[:, :FF]) * both[:, FF:]).astype(jnp.bfloat16)
        result = jnp.dot(inner, down_part, preferred_element_type=jnp.float32).astype(jnp.bfloat16)
        return (summed.at[table_row].add(result.astype(jnp.float32) * share_row[:, None]), None)
    summed, _ = lax.scan(expert_step, jnp.zeros((total + 1, D), jnp.float32), (table, shares, gate_up, down_weight))
    return (hidden_state + summed[:total]).astype(jnp.bfloat16).reshape(sequence_total, token_length, D)
```

```python
import functools

import jax
import jax.numpy as jnp
from jax import lax
from jax.experimental import pallas as pl
from jax.experimental.pallas import tpu as pltpu
from jax.sharding import PartitionSpec as P

HEAD_WIDTH = 128
MESH = pl.DeviceIdType.MESH
CORES = 2
CHUNK = 512


def normalize_rows(scores):
    highest = jnp.max(scores, axis=-1, keepdims=True)
    raised = jnp.exp(scores - highest)
    return (raised / jnp.sum(raised, axis=-1, keepdims=True)).astype(jnp.bfloat16)


def loop(low, high, body):
    lax.fori_loop(low, high, lambda i, carry: (body(i), carry)[1], 0)


def expert_kernel(
    line, plane,
    normed, hidden, sel, share, gate_hbm, down_hbm,
    out,
    rows, packed, arrived, both, gate, down, inner, returned, own, part_out, part_in,
    line_s1, line_r1, plane_s1, plane_r1, plane_s2, plane_r2, line_s2, line_r2, load_sem,
):
    tokens = normed.shape[0]
    parts = rows.shape[0]
    slots = sel.shape[0] // plane
    half = gate.shape[1] // 2
    group = lax.axis_index("grp")
    place = lax.axis_index("seq")
    z, core = place // CORES, place % CORES
    me = group * CORES + core

    def on_line(k):
        other = (z + k) % line
        return other, (group, other * CORES + core)

    def on_plane(k):
        other = (me + k) % plane
        return other, (other // CORES, z * CORES + other % CORES)

    def block(i):
        return pl.ds(pl.multiple_of(i * slots, 16), slots)

    def tok(i):
        return pl.ds(pl.multiple_of(i * tokens, 16), tokens)

    def columns(i, width):
        return pl.ds(pl.multiple_of(i * width, 128), width)

    def line1(c, k):
        _, device = on_line(k)
        mine = rows.at[c, tok(z)]
        return pltpu.make_async_remote_copy(
            mine, mine, line_s1.at[c, k - 1], line_r1.at[c, k - 1], device_id=device, device_id_type=MESH
        )

    def plane1(c, k):
        other, device = on_plane(k)
        return pltpu.make_async_remote_copy(
            packed.at[c, block(other)], arrived.at[c, block(me)],
            plane_s1.at[c, k - 1], plane_r1.at[c, k - 1], device_id=device, device_id_type=MESH,
        )

    def plane2(c, k):
        other, device = on_plane(k)
        return pltpu.make_async_remote_copy(
            packed.at[c, block(other)], returned.at[c, block(me)],
            plane_s2.at[c, k - 1], plane_r2.at[c, k - 1], device_id=device, device_id_type=MESH,
        )

    def line2(c, k):
        other, device = on_line(k)
        return pltpu.make_async_remote_copy(
            part_out.at[c, tok(other)], part_in.at[c, k - 1],
            line_s2.at[c, k - 1], line_r2.at[c, k - 1], device_id=device, device_id_type=MESH,
        )

    load_gate = pltpu.make_async_copy(gate_hbm.at[0], gate, load_sem.at[0])
    load_down = pltpu.make_async_copy(down_hbm.at[0], down, load_sem.at[1])
    load_gate.start()
    load_down.start()

    barrier = pltpu.get_barrier_semaphore()
    for k in range(1, line):
        pl.semaphore_signal(barrier, inc=1, device_id=on_line(k)[1], device_id_type=MESH)
    for k in range(1, plane):
        pl.semaphore_signal(barrier, inc=1, device_id=on_plane(k)[1], device_id_type=MESH)
    pl.semaphore_wait(barrier, line + plane - 2)

    for c in range(parts):
        rows[c, tok(z), :] = normed[:, c * CHUNK : (c + 1) * CHUNK]
        loop(1, line, lambda k: line1(c, k).start())

    def picked(c, other):
        return jnp.dot(sel[block(other), :], rows[c], preferred_element_type=jnp.float32).astype(jnp.bfloat16)

    def pack(c):
        loop(1, line, lambda k: line1(c, k).wait_recv())

        def one(k):
            other, _ = on_plane(k)
            packed[c, block(other), :] = picked(c, other)
            plane1(c, k).start()

        loop(1, plane, one)
        arrived[c, block(me), :] = picked(c, me)

    def first(c):
        if c == 0:
            load_gate.wait()
        loop(1, plane, lambda k: plane1(c, k).wait_recv())

        def one(n):
            cols = columns(n, 256)
            term = jnp.dot(
                arrived[c], gate[c * CHUNK : (c + 1) * CHUNK, cols], preferred_element_type=jnp.float32
            )
            if c == 0:
                both[:, cols] = term
            else:
                both[:, cols] += term

        loop(0, 2 * half // 256, one)

    pack(0)
    for c in range(1, parts):
        pack(c)
        first(c - 1)
    first(parts - 1)

    def activate(i):
        g = both[block(i), :half]
        inner[block(i), :] = (g / (1.0 + jnp.exp(-g)) * both[block(i), half:]).astype(jnp.bfloat16)

    loop(0, plane, activate)
    load_down.wait()

    for c in range(parts):
        loop(1, plane, lambda k: plane1(c, k).wait_send())

        def second(n):
            packed[c, :, columns(n, 256)] = jnp.dot(
                inner[...], down[:, columns(n + c * (CHUNK // 256), 256)], preferred_element_type=jnp.float32
            ).astype(jnp.bfloat16)

        loop(0, CHUNK // 256, second)
        loop(1, plane, lambda k: plane2(c, k).start())
        returned[c, block(me), :] = packed[c, block(me), :]

    for c in range(parts):
        loop(1, plane, lambda k: plane2(c, k).wait_recv())

        def summed(other):
            return jnp.dot(share[tok(other), :], returned[c], preferred_element_type=jnp.float32)

        def send(k):
            other, _ = on_line(k)
            part_out[c, tok(other), :] = summed(other).astype(jnp.bfloat16)
            line2(c, k).start()

        loop(1, line, send)
        own[c] = summed(z)

    for c in range(parts):
        loop(1, line, lambda k: line2(c, k).wait_recv())
        total = hidden[:, c * CHUNK : (c + 1) * CHUNK] + own[c]
        for k in range(1, line):
            total += part_in[c, k - 1].astype(jnp.float32)
        out[:, c * CHUNK : (c + 1) * CHUNK] = total.astype(jnp.bfloat16)

    for c in range(parts):
        loop(1, line, lambda k: line1(c, k).wait_send())
        loop(1, plane, lambda k: plane2(c, k).wait_send())
        loop(1, line, lambda k: line2(c, k).wait_send())


def experts(normed, hidden, sel, share, gate_up, down_weight, line, plane):
    tokens, width = normed.shape
    parts = width // CHUNK
    total, gathered = sel.shape
    half = down_weight.shape[1]
    bf16, f32 = jnp.bfloat16, jnp.float32
    vmem = pl.BlockSpec(memory_space=pltpu.VMEM)
    anywhere = pl.BlockSpec(memory_space=pl.ANY)
    dma = pltpu.SemaphoreType.DMA
    on_line, on_plane = dma((parts, line - 1)), dma((parts, plane - 1))
    return pl.pallas_call(
        functools.partial(expert_kernel, line, plane),
        out_shape=jax.ShapeDtypeStruct((tokens, width), bf16),
        in_specs=[vmem, vmem, vmem, vmem, anywhere, anywhere],
        out_specs=vmem,
        scratch_shapes=[
            pltpu.VMEM((parts, gathered, CHUNK), bf16),
            pltpu.VMEM((parts, total, CHUNK), bf16),
            pltpu.VMEM((parts, total, CHUNK), bf16),
            pltpu.VMEM((total, 2 * half), f32),
            pltpu.VMEM((width, 2 * half), bf16),
            pltpu.VMEM((half, width), bf16),
            pltpu.VMEM((total, half), bf16),
            pltpu.VMEM((parts, total, CHUNK), bf16),
            pltpu.VMEM((parts, tokens, CHUNK), f32),
            pltpu.VMEM((parts, gathered, CHUNK), bf16),
            pltpu.VMEM((parts, line - 1, tokens, CHUNK), bf16),
            on_line, on_line, on_plane, on_plane, on_plane, on_plane, on_line, on_line, dma((2,)),
        ],
        compiler_params=pltpu.CompilerParams(
            collective_id=0, has_side_effects=True, vmem_limit_bytes=60 * 2**20
        ),
        cost_estimate=pl.CostEstimate(
            flops=6 * total * width * half, bytes_accessed=6 * width * half, transcendentals=total * half
        ),
    )(normed, hidden, sel, share, gate_up, down_weight)


def routing(route_ids, route_weights, line, plane, experts_all):
    tokens, top = route_ids.shape[1:]
    n_seq = lax.axis_size("seq")
    place = lax.axis_index("seq")
    z, core = place // CORES, place % CORES
    capacity = tokens * top * 9 // (8 * experts_all)
    slots = -(-line * capacity // 16) * 16
    both = jnp.concatenate([route_ids[0].astype(jnp.float32), route_weights[0]], axis=1)
    both = lax.all_gather(both, "seq", axis=0).reshape(line, CORES, tokens, 2 * top)
    both = lax.dynamic_index_in_dim(both, core, 1, keepdims=False)
    ids, weights = both[..., :top].astype(jnp.int32), both[..., top:]
    members = jnp.arange(plane, dtype=jnp.int32)
    here = members // CORES * n_seq + z * CORES + members % CORES
    match = ids[..., None] == here
    named = jnp.any(match, axis=2)
    weight = jnp.sum(jnp.where(match, weights[..., None], 0.0), axis=2)
    order = jnp.arange(tokens)
    before = (order[None, :] < order[:, None]).astype(jnp.bfloat16)
    slot = jnp.einsum("ts,lsp->ltp", before, named.astype(jnp.bfloat16), preferred_element_type=jnp.float32)
    first = jnp.arange(line, dtype=jnp.int32)[:, None, None] * capacity
    target = jnp.where(named, slot.astype(jnp.int32) + first, -1).reshape(line * tokens, plane)
    weight = weight.reshape(line * tokens, plane)
    at = jnp.arange(slots, dtype=jnp.int32)
    sel = (target.T[:, None, :] == at[None, :, None]).astype(jnp.bfloat16)
    share = jnp.where(target[:, :, None] == at, weight[:, :, None], 0.0).astype(jnp.bfloat16)
    return sel.reshape(plane * slots, line * tokens), share.reshape(line * tokens, plane * slots)


def attention(queries, keys, values):
    token_rows = queries.shape[1]
    kv_heads = keys.shape[2] // HEAD_WIDTH
    heads_per_group = queries.shape[2] // keys.shape[2]
    whole_keys, whole_values = (
        lax.all_gather(keys, "seq", axis=1, tiled=True),
        lax.all_gather(values, "seq", axis=1, tiled=True),
    )
    token_length = whole_keys.shape[1]
    first_row = lax.axis_index("seq") * token_rows
    row_index = first_row + jnp.arange(token_rows, dtype=jnp.int32)[:, None]
    col_index = jnp.arange(token_length, dtype=jnp.int32)[None, :]
    allowed = (col_index <= row_index)[None]
    grouped = queries[0].reshape(token_rows, kv_heads, heads_per_group, HEAD_WIDTH)
    results = []
    for kv_index in range(kv_heads):
        window = slice(kv_index * HEAD_WIDTH, (kv_index + 1) * HEAD_WIDTH)
        scores = jnp.einsum(
            "tgd,kd->gtk",
            grouped[:, kv_index],
            whole_keys[0, :, window],
            preferred_element_type=jnp.float32,
        ) * HEAD_WIDTH ** (-0.5)
        scores = jnp.where(allowed, scores, -jnp.inf)
        weighted = jnp.einsum(
            "gtk,kd->tgd",
            normalize_rows(scores),
            whole_values[0, :, window],
            preferred_element_type=jnp.float32,
        ).astype(jnp.bfloat16)
        results.append(weighted.reshape(token_rows, heads_per_group * HEAD_WIDTH))
    return jnp.concatenate(results, axis=1)


def on_device(
    queries, keys, values, route_ids, route_weights, out_weight, norm_gain, gate_up, down_weight
):
    n_grp, n_seq = lax.axis_size("grp"), lax.axis_size("seq")
    line, plane = n_seq // CORES, n_grp * CORES
    sel, share = routing(route_ids, route_weights, line, plane, n_grp * n_seq)
    attended = attention(queries, keys, values)
    hidden_state = jnp.dot(attended, out_weight, preferred_element_type=jnp.float32)
    power = jnp.mean(hidden_state * hidden_state, axis=-1, keepdims=True)
    normed = (hidden_state * lax.rsqrt(power + 1e-06) * norm_gain).astype(jnp.bfloat16)
    return experts(normed, hidden_state, sel, share, gate_up, down_weight, line, plane)[None]


def solution(mesh):
    placed = (
        P("grp", "seq", None),
        P("grp", "seq", None),
        P("grp", "seq", None),
        P("grp", "seq", None),
        P("grp", "seq", None),
        P(),
        P(),
        P(("grp", "seq"), None, None),
        P(("grp", "seq"), None, None),
    )
    return jax.shard_map(
        on_device, mesh=mesh, in_specs=placed, out_specs=P("grp", "seq", None), check_vma=False
    )
```

```python
import functools

import jax
import jax.numpy as jnp
from jax import lax
from jax.experimental import pallas as pl
from jax.experimental.pallas import tpu as pltpu
from jax.sharding import PartitionSpec as P

HEAD_WIDTH = 128
MESH = pl.DeviceIdType.MESH
CORES = 2
CHUNK = 256


def loop(low, high, body):
    lax.fori_loop(low, high, lambda i, carry: (body(i), carry)[1], 0)


def expert_kernel(
    line, plane,
    normed, hidden, sel, share, gate_hbm, down_hbm,
    out,
    rows, packed, arrived, both, gate, down, inner, returned, own, part_out, part_in,
    line_s1, line_r1, plane_s1, plane_r1, plane_s2, plane_r2, line_s2, line_r2, load_sem,
):
    tokens = normed.shape[0]
    parts = rows.shape[0]
    slots = sel.shape[0] // plane
    half = gate.shape[1] // 2
    group = lax.axis_index("grp")
    place = lax.axis_index("seq")
    z, core = place // CORES, place % CORES
    me = group * CORES + core

    def on_line(k):
        other = (z + k) % line
        return other, (group, other * CORES + core)

    def on_plane(k):
        other = (me + k) % plane
        return other, (other // CORES, z * CORES + other % CORES)

    def block(i):
        return pl.ds(pl.multiple_of(i * slots, 16), slots)

    def tok(i):
        return pl.ds(pl.multiple_of(i * tokens, 16), tokens)

    def columns(i, width):
        return pl.ds(pl.multiple_of(i * width, 128), width)

    def line1(c, k):
        _, device = on_line(k)
        mine = rows.at[c, tok(z)]
        return pltpu.make_async_remote_copy(
            mine, mine, line_s1.at[c, k - 1], line_r1.at[c, k - 1], device_id=device, device_id_type=MESH
        )

    def plane1(c, k):
        other, device = on_plane(k)
        return pltpu.make_async_remote_copy(
            packed.at[c, block(other)], arrived.at[c, block(me)],
            plane_s1.at[c, k - 1], plane_r1.at[c, k - 1], device_id=device, device_id_type=MESH,
        )

    def plane2(c, k):
        other, device = on_plane(k)
        return pltpu.make_async_remote_copy(
            packed.at[c, block(other)], returned.at[c, block(me)],
            plane_s2.at[c, k - 1], plane_r2.at[c, k - 1], device_id=device, device_id_type=MESH,
        )

    def line2(c, k):
        other, device = on_line(k)
        return pltpu.make_async_remote_copy(
            part_out.at[c, tok(other)], part_in.at[c, k - 1],
            line_s2.at[c, k - 1], line_r2.at[c, k - 1], device_id=device, device_id_type=MESH,
        )

    load_gate = pltpu.make_async_copy(gate_hbm.at[0], gate, load_sem.at[0])
    load_down = pltpu.make_async_copy(down_hbm.at[0], down, load_sem.at[1])
    load_gate.start()
    load_down.start()

    barrier = pltpu.get_barrier_semaphore()
    for k in range(1, line):
        pl.semaphore_signal(barrier, inc=1, device_id=on_line(k)[1], device_id_type=MESH)
    for k in range(1, plane):
        pl.semaphore_signal(barrier, inc=1, device_id=on_plane(k)[1], device_id_type=MESH)
    pl.semaphore_wait(barrier, line + plane - 2)

    for c in range(parts):
        rows[c, tok(z), :] = normed[:, c * CHUNK : (c + 1) * CHUNK]
        loop(1, line, lambda k: line1(c, k).start())

    def picked(c, other):
        return jnp.dot(sel[block(other), :], rows[c], preferred_element_type=jnp.float32).astype(jnp.bfloat16)

    def pack(c):
        loop(1, line, lambda k: line1(c, k).wait_recv())

        def one(k):
            other, _ = on_plane(k)
            packed[c, block(other), :] = picked(c, other)
            plane1(c, k).start()

        loop(1, plane, one)
        arrived[c, block(me), :] = picked(c, me)

    def first(c):
        if c == 0:
            load_gate.wait()
        loop(1, plane, lambda k: plane1(c, k).wait_recv())

        def one(n):
            cols = columns(n, 256)
            term = jnp.dot(
                arrived[c], gate[c * CHUNK : (c + 1) * CHUNK, cols], preferred_element_type=jnp.float32
            )
            if c == 0:
                both[:, cols] = term
            else:
                both[:, cols] += term

        loop(0, 2 * half // 256, one)

    pack(0)
    for c in range(1, parts):
        pack(c)
        first(c - 1)
    first(parts - 1)

    def activate(i):
        g = both[block(i), :half]
        inner[block(i), :] = (g / (1.0 + jnp.exp(-g)) * both[block(i), half:]).astype(jnp.bfloat16)

    loop(0, plane, activate)
    load_down.wait()

    for c in range(parts):
        loop(1, plane, lambda k: plane1(c, k).wait_send())

        def second(n):
            packed[c, :, columns(n, 256)] = jnp.dot(
                inner[...], down[:, columns(n + c * (CHUNK // 256), 256)], preferred_element_type=jnp.float32
            ).astype(jnp.bfloat16)

        loop(0, CHUNK // 256, second)
        loop(1, plane, lambda k: plane2(c, k).start())
        returned[c, block(me), :] = packed[c, block(me), :]

    for c in range(parts):
        loop(1, plane, lambda k: plane2(c, k).wait_recv())

        def summed(other):
            return jnp.dot(share[tok(other), :], returned[c], preferred_element_type=jnp.float32)

        def send(k):
            other, _ = on_line(k)
            part_out[c, tok(other), :] = summed(other).astype(jnp.bfloat16)
            line2(c, k).start()

        loop(1, line, send)
        own[c] = summed(z)

    for c in range(parts):
        loop(1, line, lambda k: line2(c, k).wait_recv())
        total = hidden[:, c * CHUNK : (c + 1) * CHUNK] + own[c]
        for k in range(1, line):
            total += part_in[c, k - 1].astype(jnp.float32)
        out[:, c * CHUNK : (c + 1) * CHUNK] = total.astype(jnp.bfloat16)

    for c in range(parts):
        loop(1, line, lambda k: line1(c, k).wait_send())
        loop(1, plane, lambda k: plane2(c, k).wait_send())
        loop(1, line, lambda k: line2(c, k).wait_send())


def experts(normed, hidden, sel, share, gate_up, down_weight, line, plane):
    tokens, width = normed.shape
    parts = width // CHUNK
    total, gathered = sel.shape
    half = down_weight.shape[1]
    bf16, f32 = jnp.bfloat16, jnp.float32
    vmem = pl.BlockSpec(memory_space=pltpu.VMEM)
    anywhere = pl.BlockSpec(memory_space=pl.ANY)
    dma = pltpu.SemaphoreType.DMA
    on_line, on_plane = dma((parts, line - 1)), dma((parts, plane - 1))
    return pl.pallas_call(
        functools.partial(expert_kernel, line, plane),
        out_shape=jax.ShapeDtypeStruct((tokens, width), bf16),
        in_specs=[vmem, vmem, vmem, vmem, anywhere, anywhere],
        out_specs=vmem,
        scratch_shapes=[
            pltpu.VMEM((parts, gathered, CHUNK), bf16),
            pltpu.VMEM((parts, total, CHUNK), bf16),
            pltpu.VMEM((parts, total, CHUNK), bf16),
            pltpu.VMEM((total, 2 * half), f32),
            pltpu.VMEM((width, 2 * half), bf16),
            pltpu.VMEM((half, width), bf16),
            pltpu.VMEM((total, half), bf16),
            pltpu.VMEM((parts, total, CHUNK), bf16),
            pltpu.VMEM((parts, tokens, CHUNK), f32),
            pltpu.VMEM((parts, gathered, CHUNK), bf16),
            pltpu.VMEM((parts, line - 1, tokens, CHUNK), bf16),
            on_line, on_line, on_plane, on_plane, on_plane, on_plane, on_line, on_line, dma((2,)),
        ],
        compiler_params=pltpu.CompilerParams(
            collective_id=0, has_side_effects=True, vmem_limit_bytes=60 * 2**20
        ),
        cost_estimate=pl.CostEstimate(
            flops=6 * total * width * half, bytes_accessed=6 * width * half, transcendentals=total * half
        ),
    )(normed, hidden, sel, share, gate_up, down_weight)


def attention_kernel(
    line, plane, capacity,
    queries, keys, values, ids, weights, gain, weight_hbm,
    hidden, normed, sel, share,
    kv, route, attended, weight, kv_s1, kv_r1, kv_s2, kv_r2, mate_sem, route_s, route_r, load_sem,
):
    tokens, width = queries.shape
    kv_width = keys.shape[1]
    everything = kv.shape[0]
    padded = route.shape[2] // 2
    slots = sel.shape[0] // plane
    bf16, f32 = jnp.bfloat16, jnp.float32
    group = lax.axis_index("grp")
    place = lax.axis_index("seq")
    z, core = place // CORES, place % CORES
    mate = (group, z * CORES + 1 - core)

    def tok(i):
        return pl.ds(pl.multiple_of(i * tokens, 16), tokens)

    def to(k):
        return group, ((z + k) % line) * CORES + core

    def line_kv(k):
        mine = kv.at[tok(place)]
        return pltpu.make_async_remote_copy(
            mine, mine, kv_s1.at[k - 1], kv_r1.at[k - 1], device_id=to(k), device_id_type=MESH
        )

    def mate_kv(k):
        held = kv.at[tok((z - k) * CORES + core)]
        return pltpu.make_async_remote_copy(
            held, held, kv_s2.at[k - 1], kv_r2.at[k - 1], device_id=mate, device_id_type=MESH
        )

    def own_kv():
        mine = kv.at[tok(place)]
        return pltpu.make_async_remote_copy(
            mine, mine, mate_sem.at[0], mate_sem.at[1], device_id=mate, device_id_type=MESH
        )

    def line_route(k):
        mine = route.at[z]
        return pltpu.make_async_remote_copy(
            mine, mine, route_s.at[k - 1], route_r.at[k - 1], device_id=to(k), device_id_type=MESH
        )

    load = pltpu.make_async_copy(weight_hbm, weight, load_sem)
    load.start()

    barrier = pltpu.get_barrier_semaphore()
    for k in range(1, line):
        pl.semaphore_signal(barrier, inc=1, device_id=to(k), device_id_type=MESH)
    pl.semaphore_signal(barrier, inc=1, device_id=mate, device_id_type=MESH)
    pl.semaphore_wait(barrier, line)

    kv[tok(place), :kv_width] = keys[...]
    kv[tok(place), kv_width:] = values[...]
    loop(1, line - z, lambda k: line_kv(k).start())

    @pl.when(core == 0)
    def _():
        own_kv().start()

    lanes = lax.broadcasted_iota(jnp.int32, (tokens, padded), 1)
    shares = jnp.zeros((tokens, padded), f32)
    named = jnp.zeros((tokens, padded), f32)
    for j in range(ids.shape[1]):
        match = lanes == ids[:, j : j + 1]
        shares = jnp.where(match, weights[:, j : j + 1], shares)
        named = jnp.where(match, 1.0, named)
    square = (tokens, tokens)
    before = lax.broadcasted_iota(jnp.int32, square, 1) < lax.broadcasted_iota(jnp.int32, square, 0)
    before = jnp.where(before, 1.0, 0.0).astype(bf16)
    slot = jnp.dot(before, named.astype(bf16), preferred_element_type=f32)
    route[z, :, :padded] = jnp.where(named > 0.5, slot, -1024.0).astype(bf16)
    route[z, :, padded:] = shares.astype(bf16)
    loop(1, line, lambda k: line_route(k).start())

    def clear(i):
        kv[tok(i), :] = jnp.zeros((tokens, 2 * kv_width), bf16)

    loop(place + 1, everything // tokens, clear)

    n_seq = line * CORES
    total = plane * slots
    q = lax.broadcasted_iota(jnp.int32, (1, total), 1)
    expert, row = q * 0 + z * CORES, q
    for i in range(1, plane):
        past = q >= i * slots
        expert = expert + jnp.where(past, 1 if i % CORES else n_seq - CORES + 1, 0)
        row = row - jnp.where(past, slots, 0)
    spread = jnp.where(lax.broadcasted_iota(jnp.int32, (padded, total), 0) == expert, 1.0, 0.0).astype(bf16)
    row = row.astype(f32)
    down_rows = lax.broadcasted_iota(jnp.int32, (slots, tokens), 0).astype(f32)
    pick_lanes = lax.broadcasted_iota(jnp.int32, (slots, padded), 1)

    loop(1, line, lambda k: line_route(k).wait_recv())
    for l in range(line):
        at = jnp.dot(route[l, :, :padded], spread, preferred_element_type=f32)
        part = jnp.dot(route[l, :, padded:], spread, preferred_element_type=f32)
        share[l * tokens : (l + 1) * tokens, :] = jnp.where(at + l * capacity == row, part, 0.0).astype(bf16)

    def choose(p):
        pick = p // CORES * n_seq + z * CORES + p % CORES
        pick = jnp.where(pick_lanes == pick, 1.0, 0.0).astype(bf16)
        for l in range(line):
            at = lax.dot_general(
                pick, route[l, :, :padded], (((1,), (1,)), ((), ())), preferred_element_type=f32
            )
            sel[pl.ds(pl.multiple_of(p * slots, 16), slots), l * tokens : (l + 1) * tokens] = jnp.where(
                at + l * capacity == down_rows, 1.0, 0.0
            ).astype(bf16)

    loop(0, plane, choose)

    def forward(k):
        line_kv(k).wait_recv()
        mate_kv(k).start()

    loop(1, z + 1, forward)
    loop(1, z + 1, lambda k: mate_kv(k).wait_recv())

    @pl.when(core == 1)
    def _():
        own_kv().wait_recv()

    heads = width // kv_width
    shape = (heads * tokens, everything)
    allowed = lax.broadcasted_iota(jnp.int32, shape, 1) <= (
        lax.rem(lax.broadcasted_iota(jnp.int32, shape, 0), tokens) + place * tokens
    )

    def head_group(g):
        def lane(h):
            return pl.ds(pl.multiple_of((g * heads + h) * HEAD_WIDTH, HEAD_WIDTH), HEAD_WIDTH)

        query = jnp.concatenate([queries[:, lane(h)] for h in range(heads)], axis=0)
        key_rows = kv[:, pl.ds(pl.multiple_of(g * HEAD_WIDTH, HEAD_WIDTH), HEAD_WIDTH)]
        value_rows = kv[:, pl.ds(pl.multiple_of(kv_width + g * HEAD_WIDTH, HEAD_WIDTH), HEAD_WIDTH)]
        scores = lax.dot_general(query, key_rows, (((1,), (1,)), ((), ())), preferred_element_type=f32)
        scores = jnp.where(allowed, scores * HEAD_WIDTH ** (-0.5), -jnp.inf)
        raised = jnp.exp(scores - jnp.max(scores, axis=-1, keepdims=True))
        scale = 1.0 / jnp.sum(raised, axis=-1, keepdims=True)
        weighted = jnp.dot((raised * scale).astype(bf16), value_rows, preferred_element_type=f32).astype(bf16)
        for h in range(heads):
            attended[:, lane(h)] = weighted[h * tokens : (h + 1) * tokens]

    loop(0, kv_width // HEAD_WIDTH, head_group)
    load.wait()

    def project(n):
        cols = pl.ds(pl.multiple_of(n * 256, 128), 256)
        hidden[:, cols] = jnp.dot(attended[...], weight[:, cols], preferred_element_type=f32)

    loop(0, width // 256, project)
    power = jnp.mean(hidden[...] * hidden[...], axis=-1, keepdims=True)
    normed[...] = (hidden[...] * lax.rsqrt(power + 1e-06) * gain[...]).astype(bf16)

    loop(1, line - z, lambda k: line_kv(k).wait_send())
    loop(1, z + 1, lambda k: mate_kv(k).wait_send())
    loop(1, line, lambda k: line_route(k).wait_send())

    @pl.when(core == 0)
    def _():
        own_kv().wait_send()


def attention(queries, keys, values, ids, weights, gain, out_weight, line, plane, experts_all):
    tokens, width = queries.shape
    kv_width = keys.shape[1]
    capacity = tokens * ids.shape[1] * 9 // (8 * experts_all)
    slots = -(-line * capacity // 16) * 16
    padded = -(-experts_all // 128) * 128
    everything = line * CORES * tokens
    bf16, f32 = jnp.bfloat16, jnp.float32
    vmem = pl.BlockSpec(memory_space=pltpu.VMEM)
    dma = pltpu.SemaphoreType.DMA
    steps = dma((line - 1,))
    return pl.pallas_call(
        functools.partial(attention_kernel, line, plane, capacity),
        out_shape=(
            jax.ShapeDtypeStruct((tokens, width), f32),
            jax.ShapeDtypeStruct((tokens, width), bf16),
            jax.ShapeDtypeStruct((plane * slots, line * tokens), bf16),
            jax.ShapeDtypeStruct((line * tokens, plane * slots), bf16),
        ),
        in_specs=[vmem] * 6 + [pl.BlockSpec(memory_space=pl.ANY)],
        out_specs=(vmem,) * 4,
        scratch_shapes=[
            pltpu.VMEM((everything, 2 * kv_width), bf16),
            pltpu.VMEM((line, tokens, 2 * padded), bf16),
            pltpu.VMEM((tokens, width), bf16),
            pltpu.VMEM((width, width), bf16),
            steps, steps, steps, steps, dma((2,)), steps, steps, dma,
        ],
        compiler_params=pltpu.CompilerParams(
            collective_id=1, has_side_effects=True, vmem_limit_bytes=56 * 2**20
        ),
        cost_estimate=pl.CostEstimate(
            flops=2 * tokens * width * (width + 2 * everything),
            bytes_accessed=2 * width * width,
            transcendentals=tokens * everything * width // HEAD_WIDTH,
        ),
    )(queries, keys, values, ids, weights, gain, out_weight)


def on_device(
    queries, keys, values, route_ids, route_weights, out_weight, norm_gain, gate_up, down_weight
):
    n_grp, n_seq = lax.axis_size("grp"), lax.axis_size("seq")
    line, plane = n_seq // CORES, n_grp * CORES
    hidden_state, normed, sel, share = attention(
        queries[0], keys[0], values[0], route_ids[0], route_weights[0], norm_gain[None], out_weight,
        line, plane, n_grp * n_seq,
    )
    return experts(normed, hidden_state, sel, share, gate_up, down_weight, line, plane)[None]


def solution(mesh):
    placed = (
        P("grp", "seq", None),
        P("grp", "seq", None),
        P("grp", "seq", None),
        P("grp", "seq", None),
        P("grp", "seq", None),
        P(),
        P(),
        P(("grp", "seq"), None, None),
        P(("grp", "seq"), None, None),
    )
    return jax.shard_map(
        on_device, mesh=mesh, in_specs=placed, out_specs=P("grp", "seq", None), check_vma=False
    )
```

```python
import functools

import jax
import jax.numpy as jnp
from jax import lax
from jax.experimental import pallas as pl
from jax.experimental.pallas import tpu as pltpu
from jax.sharding import PartitionSpec as P

HEAD_WIDTH = 128
MESH = pl.DeviceIdType.MESH
CORES = 2
CHUNK = 256


def loop(low, high, body):
    lax.fori_loop(low, high, lambda i, carry: (body(i), carry)[1], 0)


def expert_kernel(
    line, plane,
    normed, hidden, sel, share, gate_hbm, down_hbm,
    out,
    rows, packed, arrived, both, gate, down, inner, returned, own, part_out, part_in,
    line_s1, line_r1, plane_s1, plane_r1, plane_s2, plane_r2, line_s2, line_r2, load_sem,
):
    tokens = normed.shape[0]
    parts = rows.shape[0]
    slots = sel.shape[0] // plane
    half = gate.shape[1] // 2
    group = lax.axis_index("grp")
    place = lax.axis_index("seq")
    z, core = place // CORES, place % CORES
    me = group * CORES + core

    def on_line(k):
        other = (z + k) % line
        return other, (group, other * CORES + core)

    def on_plane(k):
        other = (me + k) % plane
        return other, (other // CORES, z * CORES + other % CORES)

    def block(i):
        return pl.ds(pl.multiple_of(i * slots, 16), slots)

    def tok(i):
        return pl.ds(pl.multiple_of(i * tokens, 16), tokens)

    def columns(i, width):
        return pl.ds(pl.multiple_of(i * width, 128), width)

    def line1(c, k):
        _, device = on_line(k)
        mine = rows.at[c, tok(z)]
        return pltpu.make_async_remote_copy(
            mine, mine, line_s1.at[c, k - 1], line_r1.at[c, k - 1], device_id=device, device_id_type=MESH
        )

    def plane1(c, k):
        other, device = on_plane(k)
        return pltpu.make_async_remote_copy(
            packed.at[c, block(other)], arrived.at[c, block(me)],
            plane_s1.at[c, k - 1], plane_r1.at[c, k - 1], device_id=device, device_id_type=MESH,
        )

    def plane2(c, k):
        other, device = on_plane(k)
        return pltpu.make_async_remote_copy(
            packed.at[c, block(other)], returned.at[c, block(me)],
            plane_s2.at[c, k - 1], plane_r2.at[c, k - 1], device_id=device, device_id_type=MESH,
        )

    def line2(c, k):
        other, device = on_line(k)
        return pltpu.make_async_remote_copy(
            part_out.at[c, tok(other)], part_in.at[c, k - 1],
            line_s2.at[c, k - 1], line_r2.at[c, k - 1], device_id=device, device_id_type=MESH,
        )

    load_gate = pltpu.make_async_copy(gate_hbm.at[0], gate, load_sem.at[0])
    load_down = pltpu.make_async_copy(down_hbm.at[0], down, load_sem.at[1])
    load_gate.start()
    load_down.start()

    barrier = pltpu.get_barrier_semaphore()
    for k in range(1, line):
        pl.semaphore_signal(barrier, inc=1, device_id=on_line(k)[1], device_id_type=MESH)
    for k in range(1, plane):
        pl.semaphore_signal(barrier, inc=1, device_id=on_plane(k)[1], device_id_type=MESH)
    pl.semaphore_wait(barrier, line + plane - 2)

    for c in range(parts):
        rows[c, tok(z), :] = normed[:, c * CHUNK : (c + 1) * CHUNK]
        loop(1, line, lambda k: line1(c, k).start())

    def picked(c, other):
        return jnp.dot(sel[block(other), :], rows[c], preferred_element_type=jnp.float32).astype(jnp.bfloat16)

    def pack(c):
        loop(1, line, lambda k: line1(c, k).wait_recv())

        def one(k):
            other, _ = on_plane(k)
            packed[c, block(other), :] = picked(c, other)
            plane1(c, k).start()

        loop(1, plane, one)
        arrived[c, block(me), :] = picked(c, me)

    def first(c):
        if c == 0:
            load_gate.wait()
        loop(1, plane, lambda k: plane1(c, k).wait_recv())

        def one(n):
            cols = columns(n, 256)
            term = jnp.dot(
                arrived[c], gate[c * CHUNK : (c + 1) * CHUNK, cols], preferred_element_type=jnp.float32
            )
            if c == 0:
                both[:, cols] = term
            else:
                both[:, cols] += term

        loop(0, 2 * half // 256, one)

    ahead = min(2, parts)
    for c in range(ahead):
        pack(c)
    for c in range(parts):
        if c + ahead < parts:
            pack(c + ahead)
        first(c)

    def activate(i):
        g = both[block(i), :half]
        inner[block(i), :] = (g / (1.0 + jnp.exp(-g)) * both[block(i), half:]).astype(jnp.bfloat16)

    loop(0, plane, activate)
    load_down.wait()

    for c in range(parts):
        loop(1, plane, lambda k: plane1(c, k).wait_send())

        def second(n):
            packed[c, :, columns(n, 256)] = jnp.dot(
                inner[...], down[:, columns(n + c * (CHUNK // 256), 256)], preferred_element_type=jnp.float32
            ).astype(jnp.bfloat16)

        loop(0, CHUNK // 256, second)
        loop(1, plane, lambda k: plane2(c, k).start())
        returned[c, block(me), :] = packed[c, block(me), :]

    for c in range(parts):
        loop(1, plane, lambda k: plane2(c, k).wait_recv())

        def summed(other):
            return jnp.dot(share[tok(other), :], returned[c], preferred_element_type=jnp.float32)

        def send(k):
            other, _ = on_line(k)
            part_out[c, tok(other), :] = summed(other).astype(jnp.bfloat16)
            line2(c, k).start()

        loop(1, line, send)
        own[c] = summed(z)

    for c in range(parts):
        loop(1, line, lambda k: line2(c, k).wait_recv())
        total = hidden[:, c * CHUNK : (c + 1) * CHUNK] + own[c]
        for k in range(1, line):
            total += part_in[c, k - 1].astype(jnp.float32)
        out[:, c * CHUNK : (c + 1) * CHUNK] = total.astype(jnp.bfloat16)

    for c in range(parts):
        loop(1, line, lambda k: line1(c, k).wait_send())
        loop(1, plane, lambda k: plane2(c, k).wait_send())
        loop(1, line, lambda k: line2(c, k).wait_send())


def experts(normed, hidden, sel, share, gate_up, down_weight, line, plane):
    tokens, width = normed.shape
    parts = width // CHUNK
    total, gathered = sel.shape
    half = down_weight.shape[1]
    bf16, f32 = jnp.bfloat16, jnp.float32
    vmem = pl.BlockSpec(memory_space=pltpu.VMEM)
    anywhere = pl.BlockSpec(memory_space=pl.ANY)
    dma = pltpu.SemaphoreType.DMA
    on_line, on_plane = dma((parts, line - 1)), dma((parts, plane - 1))
    return pl.pallas_call(
        functools.partial(expert_kernel, line, plane),
        out_shape=jax.ShapeDtypeStruct((tokens, width), bf16),
        in_specs=[vmem, vmem, vmem, vmem, anywhere, anywhere],
        out_specs=vmem,
        scratch_shapes=[
            pltpu.VMEM((parts, gathered, CHUNK), bf16),
            pltpu.VMEM((parts, total, CHUNK), bf16),
            pltpu.VMEM((parts, total, CHUNK), bf16),
            pltpu.VMEM((total, 2 * half), f32),
            pltpu.VMEM((width, 2 * half), bf16),
            pltpu.VMEM((half, width), bf16),
            pltpu.VMEM((total, half), bf16),
            pltpu.VMEM((parts, total, CHUNK), bf16),
            pltpu.VMEM((parts, tokens, CHUNK), f32),
            pltpu.VMEM((parts, gathered, CHUNK), bf16),
            pltpu.VMEM((parts, line - 1, tokens, CHUNK), bf16),
            on_line, on_line, on_plane, on_plane, on_plane, on_plane, on_line, on_line, dma((2,)),
        ],
        compiler_params=pltpu.CompilerParams(
            collective_id=0, has_side_effects=True, vmem_limit_bytes=60 * 2**20
        ),
        cost_estimate=pl.CostEstimate(
            flops=6 * total * width * half, bytes_accessed=6 * width * half, transcendentals=total * half
        ),
    )(normed, hidden, sel, share, gate_up, down_weight)


def attention_kernel(
    line, plane, capacity,
    queries, keys, values, ids, weights, gain, weight_hbm,
    hidden, normed, sel, share,
    kv, route, attended, weight, kv_s1, kv_r1, kv_s2, kv_r2, mate_sem, route_s, route_r, load_sem,
):
    tokens, width = queries.shape
    kv_width = keys.shape[1]
    everything = kv.shape[0]
    padded = route.shape[2] // 2
    slots = sel.shape[0] // plane
    bf16, f32 = jnp.bfloat16, jnp.float32
    group = lax.axis_index("grp")
    place = lax.axis_index("seq")
    z, core = place // CORES, place % CORES
    mate = (group, z * CORES + 1 - core)

    def tok(i):
        return pl.ds(pl.multiple_of(i * tokens, 16), tokens)

    def to(k):
        return group, ((z + k) % line) * CORES + core

    def line_kv(k):
        mine = kv.at[tok(place)]
        return pltpu.make_async_remote_copy(
            mine, mine, kv_s1.at[k - 1], kv_r1.at[k - 1], device_id=to(k), device_id_type=MESH
        )

    def mate_kv(k):
        held = kv.at[tok((z - k) * CORES + core)]
        return pltpu.make_async_remote_copy(
            held, held, kv_s2.at[k - 1], kv_r2.at[k - 1], device_id=mate, device_id_type=MESH
        )

    def own_kv():
        mine = kv.at[tok(place)]
        return pltpu.make_async_remote_copy(
            mine, mine, mate_sem.at[0], mate_sem.at[1], device_id=mate, device_id_type=MESH
        )

    def line_route(k):
        mine = route.at[z]
        return pltpu.make_async_remote_copy(
            mine, mine, route_s.at[k - 1], route_r.at[k - 1], device_id=to(k), device_id_type=MESH
        )

    load = pltpu.make_async_copy(weight_hbm, weight, load_sem)
    load.start()

    barrier = pltpu.get_barrier_semaphore()
    for k in range(1, line):
        pl.semaphore_signal(barrier, inc=1, device_id=to(k), device_id_type=MESH)
    pl.semaphore_signal(barrier, inc=1, device_id=mate, device_id_type=MESH)
    pl.semaphore_wait(barrier, line)

    kv[tok(place), :kv_width] = keys[...]
    kv[tok(place), kv_width:] = values[...]
    loop(1, line - z, lambda k: line_kv(k).start())

    @pl.when(core == 0)
    def _():
        own_kv().start()

    lanes = lax.broadcasted_iota(jnp.int32, (tokens, padded), 1)
    shares = jnp.zeros((tokens, padded), f32)
    named = jnp.zeros((tokens, padded), f32)
    for j in range(ids.shape[1]):
        match = lanes == ids[:, j : j + 1]
        shares = jnp.where(match, weights[:, j : j + 1], shares)
        named = jnp.where(match, 1.0, named)
    square = (tokens, tokens)
    before = lax.broadcasted_iota(jnp.int32, square, 1) < lax.broadcasted_iota(jnp.int32, square, 0)
    before = jnp.where(before, 1.0, 0.0).astype(bf16)
    slot = jnp.dot(before, named.astype(bf16), preferred_element_type=f32)
    route[z, :, :padded] = jnp.where(named > 0.5, slot, -1024.0).astype(bf16)
    route[z, :, padded:] = shares.astype(bf16)
    loop(1, line, lambda k: line_route(k).start())

    def clear(i):
        kv[tok(i), :] = jnp.zeros((tokens, 2 * kv_width), bf16)

    loop(place + 1, everything // tokens, clear)

    n_seq = line * CORES
    total = plane * slots
    q = lax.broadcasted_iota(jnp.int32, (1, total), 1)
    expert, row = q * 0 + z * CORES, q
    for i in range(1, plane):
        past = q >= i * slots
        expert = expert + jnp.where(past, 1 if i % CORES else n_seq - CORES + 1, 0)
        row = row - jnp.where(past, slots, 0)
    spread = jnp.where(lax.broadcasted_iota(jnp.int32, (padded, total), 0) == expert, 1.0, 0.0).astype(bf16)
    row = row.astype(f32)
    down_rows = lax.broadcasted_iota(jnp.int32, (slots, tokens), 0).astype(f32)
    pick_lanes = lax.broadcasted_iota(jnp.int32, (slots, padded), 1)

    loop(1, line, lambda k: line_route(k).wait_recv())
    for l in range(line):
        at = jnp.dot(route[l, :, :padded], spread, preferred_element_type=f32)
        part = jnp.dot(route[l, :, padded:], spread, preferred_element_type=f32)
        share[l * tokens : (l + 1) * tokens, :] = jnp.where(at + l * capacity == row, part, 0.0).astype(bf16)

    def choose(p):
        pick = p // CORES * n_seq + z * CORES + p % CORES
        pick = jnp.where(pick_lanes == pick, 1.0, 0.0).astype(bf16)
        for l in range(line):
            at = lax.dot_general(
                pick, route[l, :, :padded], (((1,), (1,)), ((), ())), preferred_element_type=f32
            )
            sel[pl.ds(pl.multiple_of(p * slots, 16), slots), l * tokens : (l + 1) * tokens] = jnp.where(
                at + l * capacity == down_rows, 1.0, 0.0
            ).astype(bf16)

    loop(0, plane, choose)

    def forward(k):
        line_kv(k).wait_recv()
        mate_kv(k).start()

    loop(1, z + 1, forward)
    loop(1, z + 1, lambda k: mate_kv(k).wait_recv())

    @pl.when(core == 1)
    def _():
        own_kv().wait_recv()

    heads = width // kv_width
    shape = (heads * tokens, everything)
    allowed = lax.broadcasted_iota(jnp.int32, shape, 1) <= (
        lax.rem(lax.broadcasted_iota(jnp.int32, shape, 0), tokens) + place * tokens
    )

    def head_group(g):
        def lane(h):
            return pl.ds(pl.multiple_of((g * heads + h) * HEAD_WIDTH, HEAD_WIDTH), HEAD_WIDTH)

        query = jnp.concatenate([queries[:, lane(h)] for h in range(heads)], axis=0)
        key_rows = kv[:, pl.ds(pl.multiple_of(g * HEAD_WIDTH, HEAD_WIDTH), HEAD_WIDTH)]
        value_rows = kv[:, pl.ds(pl.multiple_of(kv_width + g * HEAD_WIDTH, HEAD_WIDTH), HEAD_WIDTH)]
        scores = lax.dot_general(query, key_rows, (((1,), (1,)), ((), ())), preferred_element_type=f32)
        scores = jnp.where(allowed, scores * HEAD_WIDTH ** (-0.5), -jnp.inf)
        raised = jnp.exp(scores - jnp.max(scores, axis=-1, keepdims=True))
        scale = 1.0 / jnp.sum(raised, axis=-1, keepdims=True)
        weighted = jnp.dot((raised * scale).astype(bf16), value_rows, preferred_element_type=f32).astype(bf16)
        for h in range(heads):
            attended[:, lane(h)] = weighted[h * tokens : (h + 1) * tokens]

    loop(0, kv_width // HEAD_WIDTH, head_group)
    load.wait()

    def project(n):
        cols = pl.ds(pl.multiple_of(n * 256, 128), 256)
        hidden[:, cols] = jnp.dot(attended[...], weight[:, cols], preferred_element_type=f32)

    loop(0, width // 256, project)
    power = jnp.mean(hidden[...] * hidden[...], axis=-1, keepdims=True)
    normed[...] = (hidden[...] * lax.rsqrt(power + 1e-06) * gain[...]).astype(bf16)

    loop(1, line - z, lambda k: line_kv(k).wait_send())
    loop(1, z + 1, lambda k: mate_kv(k).wait_send())
    loop(1, line, lambda k: line_route(k).wait_send())

    @pl.when(core == 0)
    def _():
        own_kv().wait_send()


def attention(queries, keys, values, ids, weights, gain, out_weight, line, plane, experts_all):
    tokens, width = queries.shape
    kv_width = keys.shape[1]
    capacity = tokens * ids.shape[1] * 9 // (8 * experts_all)
    slots = -(-line * capacity // 16) * 16
    padded = -(-experts_all // 128) * 128
    everything = line * CORES * tokens
    bf16, f32 = jnp.bfloat16, jnp.float32
    vmem = pl.BlockSpec(memory_space=pltpu.VMEM)
    dma = pltpu.SemaphoreType.DMA
    steps = dma((line - 1,))
    return pl.pallas_call(
        functools.partial(attention_kernel, line, plane, capacity),
        out_shape=(
            jax.ShapeDtypeStruct((tokens, width), f32),
            jax.ShapeDtypeStruct((tokens, width), bf16),
            jax.ShapeDtypeStruct((plane * slots, line * tokens), bf16),
            jax.ShapeDtypeStruct((line * tokens, plane * slots), bf16),
        ),
        in_specs=[vmem] * 6 + [pl.BlockSpec(memory_space=pl.ANY)],
        out_specs=(vmem,) * 4,
        scratch_shapes=[
            pltpu.VMEM((everything, 2 * kv_width), bf16),
            pltpu.VMEM((line, tokens, 2 * padded), bf16),
            pltpu.VMEM((tokens, width), bf16),
            pltpu.VMEM((width, width), bf16),
            steps, steps, steps, steps, dma((2,)), steps, steps, dma,
        ],
        compiler_params=pltpu.CompilerParams(
            collective_id=1, has_side_effects=True, vmem_limit_bytes=56 * 2**20
        ),
        cost_estimate=pl.CostEstimate(
            flops=2 * tokens * width * (width + 2 * everything),
            bytes_accessed=2 * width * width,
            transcendentals=tokens * everything * width // HEAD_WIDTH,
        ),
    )(queries, keys, values, ids, weights, gain, out_weight)


def on_device(
    queries, keys, values, route_ids, route_weights, out_weight, norm_gain, gate_up, down_weight
):
    n_grp, n_seq = lax.axis_size("grp"), lax.axis_size("seq")
    line, plane = n_seq // CORES, n_grp * CORES
    hidden_state, normed, sel, share = attention(
        queries[0], keys[0], values[0], route_ids[0], route_weights[0], norm_gain[None], out_weight,
        line, plane, n_grp * n_seq,
    )
    return experts(normed, hidden_state, sel, share, gate_up, down_weight, line, plane)[None]


def solution(mesh):
    placed = (
        P("grp", "seq", None),
        P("grp", "seq", None),
        P("grp", "seq", None),
        P("grp", "seq", None),
        P("grp", "seq", None),
        P(),
        P(),
        P(("grp", "seq"), None, None),
        P(("grp", "seq"), None, None),
    )
    return jax.shard_map(
        on_device, mesh=mesh, in_specs=placed, out_specs=P("grp", "seq", None), check_vma=False
    )
```
